256 devices in a mesh: segment: 32 (over y_hi, z, core), tp: 8 (over x, y_lo).
Axes of the slice: x: 4, y: 4 (y_hi: 2, y_lo: 2; y = y_hi * 2 + y_lo), z: 8, core: 2. Of those that a mesh axis runs over, the one named last changes fastest.
Arguments:
- node_rows: bfloat16 [14336, 4096], P(('segment', 'tp')), may hold values from -6 to 6
- out_grad: bfloat16 [14336, 4096], P(('segment', 'tp')), may hold values from -6 to 6
- up_blocks: bfloat16 [1792, 16, 128, 128], P(('segment', 'tp')), may hold values from -0.125 to 0.125
- down_blocks: bfloat16 [1792, 16, 128, 128], P(('segment', 'tp')), may hold values from -0.0625 to 0.0625
- block_rows: int32 [1792, 16], P(('segment', 'tp')), may hold values from 0 to 31, as said below
Outputs:
- prev_grads: bfloat16 [14336, 4096], P(('segment', 'tp'))
The draws below stay inside these ranges and needn't reach their ends.
Inputs may be any that keep to these rules, and one draw needn't show every extreme that they name: `block_rows`: each row names 16 distinct feature blocks in rising order.
All inputs are finite; a program needn't handle non-finite values.
Results may differ from the reference program's by a relative error of at most 0.015.
Values may be sent and summed in bfloat16 or wider, within the bound.
A program may use at most 192 MiB of HBM per device.

```python
import jax
import jax.numpy as jnp
from jax import lax

D = 4096
FF = 14336
BLOCK = 128
NB = 32
KEEP = 16
COLS = 112
LAYERS = 16
GROUP_ROWS = 896
ROWS = 14336
ALL_COLS = 1792


def draw_block_rows(key, part):
    scores = jax.random.randint(key, (ALL_COLS, NB), 0, 1 << 20) * NB + jnp.arange(NB)[None, :]
    order = jnp.argsort(scores, axis=1)
    chosen = jnp.sort(order[:, :KEEP], axis=1)
    return chosen.astype(jnp.int32)


def levels(rng, shape, split, smallest, largest):
    def one(position, blocks):
        steps = jax.random.uniform(jax.random.fold_in(jax.random.fold_in(rng, 6), position), (blocks,), jnp.float32, smallest / len(split), largest / len(split))
        return jnp.repeat(jnp.exp(steps), shape[position] // blocks).reshape((-1,) + (1,) * (len(shape) - position - 1))

    factor_of = one(*split[0])
    for cut in split[1:]:
        factor_of = factor_of * one(*cut)
    return factor_of


def scatter_about(stream_key, extent, deviation, bound, cuts=(), held_as=jnp.bfloat16):
    result = jax.random.normal(stream_key, extent, jnp.float32) * deviation
    if len(cuts) > 0:
        result = levels(stream_key, extent, cuts, -0.22, 0.18) * result
    return jnp.clip(result, min=-bound, max=bound).astype(held_as)


def setup_inputs(seed: int = 0) -> dict:
    seeds = jax.random.split(jax.random.key(seed), 6)
    node_rows = scatter_about(seeds[0], (ROWS, D), 1.0, 6.0, ((0, 256),))
    out_grad = scatter_about(seeds[1], (ROWS, D), 1.0, 6.0, ((0, 256),))
    up_blocks = scatter_about(seeds[2], (ALL_COLS, KEEP, BLOCK, BLOCK), (D // 2) ** -0.5, 0.125, ((0, 256),))
    down_blocks = scatter_about(seeds[3], (ALL_COLS, KEEP, BLOCK, BLOCK), (FF // 2) ** -0.5, 0.0625, ((0, 256),))
    block_rows = draw_block_rows(jax.random.fold_in(seeds[5], 71), 0)
    return dict(node_rows=node_rows, out_grad=out_grad, up_blocks=up_blocks, down_blocks=down_blocks, block_rows=block_rows)


EPSILON = 1e-05

def layer_grad(node_layer, grad_layer, up_layer, down_layer, rows_layer):
    row_count = node_layer.shape[0]
    values = node_layer.astype(jnp.float32)
    inv_rms = lax.rsqrt(lax.optimization_barrier(jnp.mean(values * values, axis=-1, keepdims=True)) + EPSILON)
    normed = (values * inv_rms).astype(jnp.bfloat16)
    normed_blocks = normed.reshape(row_count, NB, BLOCK).astype(jnp.float32)
    grad_blocks = grad_layer.reshape(row_count, NB, BLOCK).astype(jnp.float32)

    def column_step(total_grad, column):
        up_col, down_col, rows_col = column
        up_wide = up_col.astype(jnp.float32)
        preact = jnp.einsum('rkb,kbe->re', normed_blocks[:, rows_col], up_wide)
        hidden_grad = jnp.einsum('rke,kfe->rf', grad_blocks[:, rows_col], down_col.astype(jnp.float32))
        sigmoid_value = jax.nn.sigmoid(preact)
        slope_grad = (hidden_grad * sigmoid_value * (1.0 + preact * (1.0 - sigmoid_value))).astype(jnp.bfloat16)
        slope_grad = lax.optimization_barrier(slope_grad)
        spread = jnp.einsum('rf,kbf->rkb', slope_grad.astype(jnp.float32), up_wide)
        return (total_grad.at[:, rows_col].add(spread), None)
    start_grad = jnp.zeros((row_count, NB, BLOCK), jnp.float32)
    normal_grad, _ = lax.scan(column_step, start_grad, (up_layer, down_layer, rows_layer))
    normal_grad = normal_grad.reshape(row_count, D)
    mixed = lax.optimization_barrier(jnp.mean(normal_grad * values, axis=-1, keepdims=True))
    input_grad = grad_layer.astype(jnp.float32) + inv_rms * normal_grad - values * inv_rms * inv_rms * inv_rms * mixed
    return input_grad.astype(jnp.bfloat16)

def reference(node_rows, out_grad, up_blocks, down_blocks, block_rows):
    node_layers = node_rows.reshape(LAYERS, GROUP_ROWS, D)
    grad_layers = out_grad.reshape(LAYERS, GROUP_ROWS, D)
    up_layers = up_blocks.reshape(LAYERS, COLS, KEEP, BLOCK, BLOCK)
    down_layers = down_blocks.reshape(LAYERS, COLS, KEEP, BLOCK, BLOCK)
    rows_layers = block_rows.reshape(LAYERS, COLS, KEEP)

    def one_layer(pieces):
        return layer_grad(pieces[0], pieces[1], pieces[2], pieces[3], pieces[4])
    input_grad = lax.map(one_layer, (node_layers, grad_layers, up_layers, down_layers, rows_layers))
    shifted = jnp.concatenate([input_grad[1:], input_grad[:1]], axis=0)
    return shifted.reshape(ROWS, D)
```

```python
import functools

import jax
import jax.numpy as jnp
from jax import lax
from jax.experimental import pallas as pl
from jax.experimental.pallas import tpu as pltpu
from jax.sharding import PartitionSpec as P

EPSILON = 1e-05
MESH = pl.DeviceIdType.MESH
BF = jnp.bfloat16
F32 = jnp.float32
U = 128
HU = 16
PU = HU + 1
TP = 8

NAMES = (
    ["st", "nd", "iv", "A1", "A2", "A3a", "A3b", "B1", "B2", "C1a", "C1b", "C2a", "C2b", "C3", "C4"]
    + ["D1", "D2", "E1", "E2"]
    + [f"G{s}" for s in range(8)]
    + [f"M1_{s}" for s in range(8)]
    + ["M2_1", "M2_4", "M2_5", "M2_7", "pA", "pB6", "pB7", "mA", "mB6", "mB7"]
    + ["L0Am", "L0Ap", "L0Bp", "L0Bm", "L1Bp", "L1Bm", "R0Am", "R0Ap", "R0Bp", "R0Bm", "R1Bp", "R1Bm", "M6"]
)
SEM = {name: i for i, name in enumerate(NAMES)}
ZSEM = len(NAMES)


def cols(first, last):
    return pl.ds(first * U, (last - first) * U)


def kernel(
    rows, layers, inv_ref, node_ref, grad_ref, up_hbm, down_hbm, out_ref,
    x_ref, up_ref, down_ref, raw_up, raw_down, slope_ref, p_ref, sib_ref,
    ra_ref, rpa_ref, rpb_ref, rma_ref, rmb_ref, rl0_ref, rl1_ref, rr0_ref, rr1_ref, r6_ref,
    st_out, st_in, nd_out, nd_in, iv_out, iv_in, node_all, iv_all, fin_ref, land_ref,
    send_sem, recv_sem, local_sem,
):
    pair = 2 * rows
    hidden_blocks = raw_up.shape[0]
    features = up_ref.shape[0]
    half = features // 2
    seg, tp = lax.axis_index("segment"), lax.axis_index("tp")
    layer, core = seg // 2, seg % 2
    gx, gy = tp // 2, tp % 2

    def at_tp(x, y):
        return (seg, lax.rem(x + 4, 4) * 2 + y)

    sibling = (layer * 2 + 1 - core, tp)
    right, left = at_tp(gx + 1, gy), at_tp(gx - 1, gy)
    across = at_tp(gx, 1 - gy)
    before = lax.rem(layer + layers - 1, layers) * 2
    after = lax.rem(layer + 1, layers) * 2

    barrier = pltpu.get_barrier_semaphore()
    greet = [sibling, right, left, across]
    greet += [(before, tp), (before + 1, tp), (after, tp), (after + 1, tp)]
    for other in greet:
        pl.semaphore_signal(barrier, inc=1, device_id=other, device_id_type=MESH)

    raw = [
        pltpu.make_async_copy(up_hbm, raw_up.at[:, pl.ds(0, 16)], local_sem.at[0]),
        pltpu.make_async_copy(down_hbm, raw_down.at[:, pl.ds(0, 16)], local_sem.at[1]),
    ]
    for copy in raw:
        copy.start()

    def xs(slot, first=0, last=HU, side=0):
        return x_ref.at[:, side, slot // 2, pl.ds(pair * (slot % 2), pair), cols(first, last)]

    def ps(slot, first=0, last=PU, side=0):
        return p_ref.at[side, slot // 2, pl.ds(pair * (slot % 2), pair), cols(first, last)]

    table = {
        "st": (st_out, st_in, sibling),
        "nd": (nd_out, nd_in, sibling),
        "iv": (iv_out, iv_in, sibling),
        "A1": (xs(0), xs(3), right),
        "A2": (xs(0), xs(2), left),
        "A3a": (xs(0, 7, 16), xs(1, 7, 16), across),
        "A3b": (xs(0, 0, 7), xs(1, 0, 7), across),
        "B1": (xs(1, 7, 16), xs(5, 7, 16), right),
        "B2": (xs(1, 7, 16), xs(4, 7, 16), left),
        "C1a": (xs(3, 4, 7), xs(6, 4, 7), right),
        "C1b": (xs(3, 7, 12), xs(6, 7, 12), right),
        "C2a": (xs(2, 0, 4), xs(6, 0, 4), left),
        "C2b": (xs(2, 12, 16), xs(6, 12, 16), left),
        "C3": (xs(3, 0, 7), xs(5, 0, 7), across),
        "C4": (xs(2, 0, 7), xs(4, 0, 7), across),
        "D1": (xs(5, 7, 12), xs(7, 7, 12), right),
        "D2": (xs(4, 12, 16), xs(7, 12, 16), left),
        "E1": (xs(6, 4, 7), xs(7, 4, 7), across),
        "E2": (xs(6, 0, 4), xs(7, 0, 4), across),
        "M2_1": (ps(1, 0, 8), ra_ref.at[0], across),
        "M2_4": (ps(4, 0, 8), ra_ref.at[1], across),
        "M2_5": (ps(5, 0, 8), ra_ref.at[2], across),
        "M2_7": (ps(7, 0, 8), ra_ref.at[3], across),
        "pA": (ps(6, 4, 8), rpa_ref, right),
        "pB6": (ps(6, 8, 13), rpb_ref.at[0], right),
        "pB7": (ps(7, 8, 13), rpb_ref.at[1], right),
        "mA": (ps(6, 0, 4), rma_ref, left),
        "mB6": (ps(6, 13, 17), rmb_ref.at[0], left),
        "mB7": (ps(7, 13, 17), rmb_ref.at[1], left),
        "L0Am": (ps(2, 0, 4), rl0_ref.at[:, cols(0, 4)], right),
        "L0Ap": (ps(2, 4, 8), rl0_ref.at[:, cols(4, 8)], right),
        "L0Bp": (ps(2, 8, 13), rl0_ref.at[:, cols(8, 13)], right),
        "L0Bm": (ps(2, 13, 17), rl0_ref.at[:, cols(13, 17)], right),
        "L1Bp": (ps(4, 8, 13), rl1_ref.at[:, cols(0, 5)], right),
        "L1Bm": (ps(4, 13, 17), rl1_ref.at[:, cols(5, 9)], right),
        "R0Am": (ps(3, 0, 4), rr0_ref.at[:, cols(0, 4)], left),
        "R0Ap": (ps(3, 4, 8), rr0_ref.at[:, cols(4, 8)], left),
        "R0Bp": (ps(3, 8, 13), rr0_ref.at[:, cols(8, 13)], left),
        "R0Bm": (ps(3, 13, 17), rr0_ref.at[:, cols(13, 17)], left),
        "R1Bp": (ps(5, 8, 13), rr1_ref.at[:, cols(0, 5)], left),
        "R1Bm": (ps(5, 13, 17), rr1_ref.at[:, cols(5, 9)], left),
        "M6": (ps(1, 8, 17), r6_ref, across),
    }
    for s in range(8):
        table[f"G{s}"] = (xs(s), xs(s, side=1), sibling)
        table[f"M1_{s}"] = (ps(s, side=1), sib_ref.at[s], sibling)

    def remote(name):
        source, target, device = table[name]
        return pltpu.make_async_remote_copy(
            src_ref=source, dst_ref=target, send_sem=send_sem.at[SEM[name]],
            recv_sem=recv_sem.at[SEM[name]], device_id=device, device_id_type=MESH,
        )

    def start(*names):
        for name in names:
            remote(name).start()

    def arrived(*names):
        for name in names:
            remote(name).wait_recv()

    def grid_rows(body):
        lax.fori_loop(0, pair // 16, lambda i, _: (body(pl.ds(pl.multiple_of(i * 16, 16), 16)), 0)[1], 0)

    def add(slot, first, last, *others):
        base = pair * (slot % 2)

        def body(r):
            here = pl.ds(pl.multiple_of(r.start + base, 16), 16)
            total = p_ref[0, slot // 2, here, cols(first, last)].astype(F32)
            for ref, begin in others:
                total = total + ref[r, cols(begin, begin + last - first)].astype(F32)
            p_ref[0, slot // 2, here, cols(first, last)] = total.astype(BF)

        grid_rows(body)

    values = node_ref[...].astype(F32)
    inv_rms = lax.rsqrt(jnp.mean(values * values, axis=-1, keepdims=True) + EPSILON)
    mine = pl.ds(pl.multiple_of(core * half, half), half)
    theirs = pl.ds(pl.multiple_of((1 - core) * half, half), half)
    st_out[0, pl.ds(0, rows)] = (node_ref[:, theirs].astype(F32) * inv_rms).astype(BF)
    st_out[1, pl.ds(0, rows)] = grad_ref[:, theirs]
    pl.semaphore_wait(barrier, len(greet))
    start("st")
    nd_out[pl.ds(0, rows)] = node_ref[:, theirs]
    iv_out[...] = jnp.broadcast_to(inv_rms, iv_out.shape)
    start("nd", "iv")
    raw_up[:, 16] = jnp.zeros((hidden_blocks, U, U), BF)
    raw_down[:, 16] = jnp.zeros((hidden_blocks, U, U), BF)

    def both(own, other):
        own, other = own.astype(F32), other.astype(F32)
        first = core == 0
        return jnp.concatenate([jnp.where(first, own, other), jnp.where(first, other, own)], axis=0)

    arrived("st")
    own_normed = node_ref[:, mine].astype(F32) * inv_rms
    x_ref[0, 0, 0, pl.ds(0, pair)] = both(own_normed.astype(BF), st_in[0, pl.ds(0, rows)]).astype(BF)
    x_ref[1, 0, 0, pl.ds(0, pair)] = both(grad_ref[:, mine], st_in[1, pl.ds(0, rows)]).astype(BF)
    start("A1", "A2", "A3a", "A3b", "G0")
    arrived("nd", "iv")
    node_all[...] = both(node_ref[:, mine], nd_in[pl.ds(0, rows)]).astype(BF)
    iv_all[...] = both(iv_out[...], iv_in[...])

    for copy in raw:
        copy.wait()

    def densify(first, last):
        def body(i, _):
            c, f = i // 32, i % 32
            kept = inv_ref[c, lax.rem(f + core * 16, 32)]
            row = pl.ds(pl.multiple_of(f * U, U), U)
            col = pl.ds(pl.multiple_of(c * U, U), U)
            up_ref[row, col] = raw_up[c, kept]
            down_ref[row, col] = raw_down[c, kept].T
            return 0

        lax.fori_loop(first * 32, last * 32, body, 0)

    cut = (hidden_blocks + 1) // 2
    densify(0, cut)
    arrived("A3a")
    start("B1", "B2")
    densify(cut, hidden_blocks)
    arrived("A1", "A2", "A3b")
    start("C1a", "C2a", "C3", "C4", "C1b", "C2b", "G1", "G2", "G3")

    wide = min(512, half)

    def compute(g):
        def dot(a, b):
            return jnp.dot(a, b, preferred_element_type=F32)

        preact = dot(x_ref[0, 0, g], up_ref[pl.ds(0, half)]) + dot(x_ref[0, 1, g], up_ref[pl.ds(half, half)])
        hidden = dot(x_ref[1, 0, g], down_ref[pl.ds(0, half)]) + dot(x_ref[1, 1, g], down_ref[pl.ds(half, half)])
        s = jax.nn.sigmoid(preact)
        slope = (hidden * s * (1.0 + preact * (1.0 - s))).astype(BF)
        slope_ref[...] = slope
        row_sum = jnp.sum(slope.astype(F32) * preact, axis=-1, keepdims=True) * (1.0 / features)
        row_sum = jnp.broadcast_to(row_sum, (row_sum.shape[0], U)).astype(BF)
        p_ref[0, g, :, pl.ds(0, U)] = row_sum
        p_ref[1, g, :, pl.ds(0, U)] = row_sum
        steps = half // wide

        def body(j, _):
            w = up_ref[pl.ds(pl.multiple_of(j * wide, wide), wide), :]
            part = lax.dot_general(slope_ref[...], w, (((1,), (1,)), ((), ())), preferred_element_type=F32)
            at = pl.ds(pl.multiple_of(lax.rem(j, steps) * wide + U, U), wide)
            p_ref[j // steps, g, :, at] = part.astype(BF)
            return 0

        lax.fori_loop(0, 2 * steps, body, 0)

    def group(g, _):
        @pl.when(g == 0)
        def _():
            arrived("G0", "G1")

        @pl.when(g == 1)
        def _():
            arrived("B1", "B2")
            start("D1", "D2")
            arrived("G2", "G3")

        @pl.when(g == 2)
        def _():
            arrived("C1a", "C2a")
            start("E1", "E2")
            arrived("C3", "C4")
            start("G4", "G5")
            arrived("M1_0", "M1_1")
            add(0, 0, PU, (sib_ref.at[0], 0))
            add(1, 0, PU, (sib_ref.at[1], 0))
            arrived("C1b", "C2b")
            start("G6")
            arrived("G4", "G5")

        @pl.when(g == 3)
        def _():
            arrived("M1_2", "M1_3")
            add(2, 0, PU, (sib_ref.at[2], 0))
            add(3, 0, PU, (sib_ref.at[3], 0))
            start("M2_1", "L0Bm", "R0Bp")
            arrived("D1", "D2", "E1", "E2")
            start("G7")
            arrived("M1_4", "M1_5")
            add(4, 0, PU, (sib_ref.at[4], 0))
            add(5, 0, PU, (sib_ref.at[5], 0))
            start("M2_4", "M2_5", "L1Bm", "R1Bp")
            arrived("G6", "G7")

        compute(g)

        for k in range(4):
            @pl.when(g == k)
            def _(k=k):
                start(f"M1_{2 * k}", f"M1_{2 * k + 1}")

        return 0

    lax.fori_loop(0, 4, group, 0)

    arrived("M2_4", "M2_5")
    add(2, 0, 8, (ra_ref.at[1], 0))
    add(3, 0, 8, (ra_ref.at[2], 0))
    start("L0Am", "R0Ap")
    arrived("M1_7")
    add(7, 0, PU, (sib_ref.at[7], 0))
    start("M2_7", "pB7", "mB7")
    arrived("M1_6")
    add(6, 0, PU, (sib_ref.at[6], 0))
    start("pB6", "mB6")
    arrived("pB7")
    add(4, 8, 13, (rpb_ref.at[1], 0))
    start("L1Bp")
    arrived("mB7")
    add(5, 13, 17, (rmb_ref.at[1], 0))
    start("R1Bm")
    arrived("M2_7")
    add(6, 0, 8, (ra_ref.at[3], 0))
    start("pA", "mA")
    arrived("pB6")
    add(2, 8, 13, (rpb_ref.at[0], 0))
    start("L0Bp")
    arrived("mB6")
    add(3, 13, 17, (rmb_ref.at[0], 0))
    start("R0Bm")
    arrived("L1Bp", "L1Bm", "R1Bp", "R1Bm")
    add(1, 8, 17, (rl1_ref, 0), (rr1_ref, 0))
    start("M6")
    arrived("pA")
    add(2, 4, 8, (rpa_ref, 0))
    start("L0Ap")
    arrived("mA")
    add(3, 0, 4, (rma_ref, 0))
    start("R0Am")

    inv_all = iv_all[...]

    def finish(unit, *others):
        total = p_ref[0, 0, pl.ds(0, pair), cols(unit, unit + 1)].astype(F32)
        for ref, at in others:
            total = total + ref[:, cols(at, at + 1)].astype(F32)
        return total

    def emit(unit, total, scaled):
        at = cols(unit - 1, unit)
        result = x_ref[1, 0, 0, pl.ds(0, pair), at].astype(F32) + inv_all * total
        result = (result - node_all[:, at].astype(F32) * scaled)
        fin_ref[0, pl.ds(0, rows), at] = result[:rows].astype(BF)
        fin_ref[1, pl.ds(0, rows), at] = result[rows:].astype(BF)

    def shift(piece, first, last):
        copies = []
        for q in range(2):
            copies.append(pltpu.make_async_remote_copy(
                src_ref=fin_ref.at[q, :, cols(first, last)],
                dst_ref=land_ref.at[core, :, cols(first, last)],
                send_sem=send_sem.at[ZSEM + 2 * piece + q],
                recv_sem=recv_sem.at[ZSEM + 2 * piece + core],
                device_id=(before + q, tp), device_id_type=MESH,
            ))
        return copies

    def landed(piece, first, last, source):
        pltpu.make_async_remote_copy(
            src_ref=land_ref.at[source, :, cols(first, last)],
            dst_ref=land_ref.at[source, :, cols(first, last)],
            send_sem=send_sem.at[ZSEM + 2 * piece],
            recv_sem=recv_sem.at[ZSEM + 2 * piece + source],
            device_id=(before, tp), device_id_type=MESH,
        ).wait_recv()

    arrived("M2_1", "L0Am", "L0Ap", "R0Am", "R0Ap")
    scaled = inv_all * inv_all * finish(0, (ra_ref.at[0], 0), (rl0_ref, 0), (rr0_ref, 0))
    for unit in range(1, 8):
        emit(unit, finish(unit, (ra_ref.at[0], unit), (rl0_ref, unit), (rr0_ref, unit)), scaled)
    for copy in shift(0, 0, 7):
        copy.start()
    arrived("L0Bp", "L0Bm", "R0Bp", "R0Bm", "M6")
    for unit in range(8, 17):
        emit(unit, finish(unit, (rl0_ref, unit), (rr0_ref, unit), (r6_ref, unit - 8)), scaled)
    for copy in shift(1, 7, 16):
        copy.start()

    for piece, first, last in ((0, 0, 7), (1, 7, 16)):
        for source in range(2):
            landed(piece, first, last, source)
            at = pl.ds(source * half + first * U, (last - first) * U)
            out_ref[:, at] = land_ref[source, pl.ds(0, rows), cols(first, last)]
    for name in NAMES:
        remote(name).wait_send()
    for copy in shift(0, 0, 7) + shift(1, 7, 16):
        copy.wait_send()


def body(layers, node_rows, out_grad, up_blocks, down_blocks, block_rows):
    rows, features = node_rows.shape
    hidden_blocks, kept = block_rows.shape
    pair, half, hidden = 2 * rows, features // 2, hidden_blocks * U
    padded = (rows + 15) // 16 * 16
    wanted = block_rows[:, None, :] == jnp.arange(features // U, dtype=jnp.int32)[None, :, None]
    inverse = jnp.min(jnp.where(wanted, jnp.arange(kept, dtype=jnp.int32), kept), axis=-1)

    def vmem(*shape, dtype=BF):
        return pltpu.VMEM(shape, dtype)

    in_vmem = pl.BlockSpec(memory_space=pltpu.VMEM)
    return pl.pallas_call(
        functools.partial(kernel, rows, layers),
        out_shape=jax.ShapeDtypeStruct((rows, features), BF),
        in_specs=[
            pl.BlockSpec(memory_space=pltpu.SMEM), in_vmem, in_vmem,
            pl.BlockSpec(memory_space=pl.ANY), pl.BlockSpec(memory_space=pl.ANY),
        ],
        out_specs=in_vmem,
        scratch_shapes=[
            vmem(2, 2, 4, 2 * pair, half),
            vmem(features, hidden),
            vmem(features, hidden),
            vmem(hidden_blocks, kept + 1, U, U),
            vmem(hidden_blocks, kept + 1, U, U),
            vmem(2 * pair, hidden),
            vmem(2, 4, 2 * pair, PU * U),
            vmem(8, pair, PU * U),
            vmem(4, pair, 8 * U),
            vmem(pair, 4 * U),
            vmem(2, pair, 5 * U),
            vmem(pair, 4 * U),
            vmem(2, pair, 4 * U),
            vmem(pair, PU * U),
            vmem(pair, 9 * U),
            vmem(pair, PU * U),
            vmem(pair, 9 * U),
            vmem(pair, 9 * U),
            vmem(2, padded, half),
            vmem(2, padded, half),
            vmem(padded, half),
            vmem(padded, half),
            vmem(rows, U, dtype=F32),
            vmem(rows, U, dtype=F32),
            vmem(pair, half),
            vmem(pair, U, dtype=F32),
            vmem(2, padded, half),
            vmem(2, padded, half),
            pltpu.SemaphoreType.DMA((ZSEM + 4,)),
            pltpu.SemaphoreType.DMA((ZSEM + 4,)),
            pltpu.SemaphoreType.DMA((2,)),
        ],
        compiler_params=pltpu.CompilerParams(
            collective_id=0, has_side_effects=True, vmem_limit_bytes=60 * 2**20
        ),
        name="layer_grad",
    )(inverse, node_rows, out_grad, up_blocks, down_blocks)


def solution(mesh):
    layers = mesh.shape["segment"] // 2
    return jax.shard_map(
        functools.partial(body, layers),
        mesh=mesh,
        in_specs=(
            P(("segment", "tp"), None),
            P(("segment", "tp"), None),
            P(("segment", "tp"), None, None, None),
            P(("segment", "tp"), None, None, None),
            P(("segment", "tp"), None),
        ),
        out_specs=P(("segment", "tp"), None),
        check_vma=False,
    )
```

```python
import functools

import jax
import jax.numpy as jnp
from jax import lax
from jax.experimental import pallas as pl
from jax.experimental.pallas import tpu as pltpu
from jax.sharding import PartitionSpec as P

EPSILON = 1e-05
MESH = pl.DeviceIdType.MESH
BF = jnp.bfloat16
F32 = jnp.float32
U = 128
HU = 16
PU = HU + 1
TP = 8

PARTS = {
    "Ama": (0, 2), "Apa": (2, 4), "Amb": (4, 6), "Apb": (6, 8),
    "Bpa": (8, 11), "Bma": (11, 13), "Bpb": (13, 15), "Bmb": (15, 17),
}
AP, AM, BP, BM = ("Apa", "Apb"), ("Ama", "Amb"), ("Bpa", "Bpb"), ("Bma", "Bmb")


def named(head, *groups):
    return [head + part for group in groups for part in group]


NAMES = (
    ["sn", "sg", "nd", "iv", "A1", "A2", "A3a", "A3b", "B1f", "B1r", "B2f", "B2r", "C1a", "C1b", "C2a", "C2b", "C3", "C4"]
    + ["D1", "D2", "E1", "E2", "G7a", "G7b"]
    + [f"G{s}" for s in range(7)]
    + [f"M1_{s}" for s in range(8)]
    + ["M2_1", "M2_4", "M2_5", "M2_7", "M6a", "M6b"]
    + named("p6", AP, BP) + named("p7", BP) + named("m6", AM, BM) + named("m7", BM)
    + named("L0", AM, AP, BP, BM) + named("L1", BP, BM) + named("R0", AM, AP, BP, BM) + named("R1", BP, BM)
)
SEM = {name: i for i, name in enumerate(NAMES)}
ZSEM = len(NAMES)


def cols(first, last):
    return pl.ds(first * U, (last - first) * U)


def kernel(
    rows, layers, kept_ref, node_ref, grad_ref, up_hbm, down_hbm, out_ref,
    x_ref, up_ref, down_ref, raw_up, raw_down, slope_ref, p_ref, sib_ref,
    r6x_ref, r7x_ref, rl0_ref, rl1_ref, rr0_ref, rr1_ref, r6_ref,
    lent_ref, given_ref, iv_out, iv_in, node_all, iv_all, fin_ref, land_ref,
    send_sem, recv_sem, local_sem, ready_sem,
):
    pair = 2 * rows
    hidden_blocks = raw_up.shape[0]
    features = up_ref.shape[0]
    half = features // 2
    seg, tp = lax.axis_index("segment"), lax.axis_index("tp")
    layer, core = seg // 2, seg % 2
    gx, gy = tp // 2, tp % 2

    def at_tp(x, y):
        return (seg, lax.rem(x + 4, 4) * 2 + y)

    sibling = (layer * 2 + 1 - core, tp)
    right, left = at_tp(gx + 1, gy), at_tp(gx - 1, gy)
    across = at_tp(gx, 1 - gy)
    before = lax.rem(layer + layers - 1, layers) * 2
    after = lax.rem(layer + 1, layers) * 2

    barrier = pltpu.get_barrier_semaphore()
    greet = [sibling, right, left, across, (before, tp), (before + 1, tp)]
    for other in greet:
        pl.semaphore_signal(barrier, inc=1, device_id=other, device_id_type=MESH)

    load_up = pltpu.make_async_copy(up_hbm, raw_up.at[:, pl.ds(0, 16)], local_sem.at[0])
    load_down = pltpu.make_async_copy(down_hbm, raw_down.at[:, pl.ds(0, 16)], local_sem.at[1])
    load_up.start()
    load_down.start()

    def xs(slot, first=0, last=HU, side=0):
        return x_ref.at[:, side, pl.ds(pair * slot, pair), cols(first, last)]

    def ps(slot, first=0, last=PU, side=0):
        return p_ref.at[side, pl.ds(pair * slot, pair), cols(first, last)]

    padded = (rows + 15) // 16 * 16
    table = {
        "sn": (lent_ref.at[0], given_ref.at[0], sibling),
        "sg": (lent_ref.at[1], given_ref.at[1], sibling),
        "nd": (lent_ref.at[2], given_ref.at[2], sibling),
        "iv": (iv_out, iv_in, sibling),
        "A1": (xs(0), xs(3), right),
        "A2": (xs(0), xs(2), left),
        "A3a": (xs(0, 7, 16), xs(1, 7, 16), across),
        "A3b": (xs(0, 0, 7), xs(1, 0, 7), across),
        "B1f": (xs(1, 7, 12), xs(5, 7, 12), right),
        "B1r": (xs(1, 12, 16), xs(5, 12, 16), right),
        "B2f": (xs(1, 12, 16), xs(4, 12, 16), left),
        "B2r": (xs(1, 7, 12), xs(4, 7, 12), left),
        "C1a": (xs(3, 4, 7), xs(6, 4, 7), right),
        "C1b": (xs(3, 7, 12), xs(6, 7, 12), right),
        "C2a": (xs(2, 0, 4), xs(6, 0, 4), left),
        "C2b": (xs(2, 12, 16), xs(6, 12, 16), left),
        "C3": (xs(3, 0, 7), xs(5, 0, 7), across),
        "C4": (xs(2, 0, 7), xs(4, 0, 7), across),
        "D1": (xs(5, 7, 12), xs(7, 7, 12), right),
        "D2": (xs(4, 12, 16), xs(7, 12, 16), left),
        "E1": (xs(6, 4, 7), xs(7, 4, 7), across),
        "E2": (xs(6, 0, 4), xs(7, 0, 4), across),
        "M2_1": (ps(1, 0, 8), rl1_ref.at[:, cols(0, 8)], across),
        "M2_4": (ps(4, 0, 8), rr1_ref.at[:, cols(0, 8)], across),
        "M2_5": (ps(5, 0, 8), r7x_ref.at[:, cols(0, 8)], across),
        "M2_7": (ps(7, 0, 8), r6_ref.at[:, cols(0, 8)], across),
        "M6a": (ps(1, 8, 13), r6_ref.at[:, cols(8, 13)], across),
        "M6b": (ps(1, 13, 17), r6_ref.at[:, cols(13, 17)], across),
        "G7a": (xs(7, 0, 7), xs(7, 0, 7, side=1), sibling),
        "G7b": (xs(7, 7, 16), xs(7, 7, 16, side=1), sibling),
    }

    def along(head, slot, target, device, *groups):
        for part in [part for group in groups for part in group]:
            table[head + part] = (ps(slot, *PARTS[part]), target.at[:, cols(*PARTS[part])], device)

    along("p6", 6, r6x_ref, right, AP, BP)
    along("p7", 7, r7x_ref, right, BP)
    along("m6", 6, r6x_ref, left, AM, BM)
    along("m7", 7, r7x_ref, left, BM)
    along("L0", 2, rl0_ref, right, AM, AP, BP, BM)
    along("L1", 4, rl1_ref, right, BP, BM)
    along("R0", 3, rr0_ref, left, AM, AP, BP, BM)
    along("R1", 5, rr1_ref, left, BP, BM)
    for s in range(8):
        if s < 7:
            table[f"G{s}"] = (xs(s), xs(s, side=1), sibling)
        table[f"M1_{s}"] = (ps(s, side=1), sib_ref.at[s], sibling)

    def remote(name):
        source, target, device = table[name]
        return pltpu.make_async_remote_copy(
            src_ref=source, dst_ref=target, send_sem=send_sem.at[SEM[name]],
            recv_sem=recv_sem.at[SEM[name]], device_id=device, device_id_type=MESH,
        )

    def start(*names):
        for name in names:
            remote(name).start()

    def arrived(*names):
        for name in names:
            remote(name).wait_recv()

    def grid_rows(body):
        lax.fori_loop(0, pair // 16, lambda i, _: (body(pl.ds(pl.multiple_of(i * 16, 16), 16)), 0)[1], 0)

    def add(slot, first, last, *others):
        def body(r):
            here = pl.ds(pl.multiple_of(r.start + pair * slot, 16), 16)
            total = p_ref[0, here, cols(first, last)].astype(F32)
            for ref in others:
                total = total + ref[r, cols(first, last)].astype(F32)
            p_ref[0, here, cols(first, last)] = total.astype(BF)

        grid_rows(body)

    def add_sibling(*slots):
        for slot in slots:
            arrived(f"M1_{slot}")
            add(slot, 0, PU, sib_ref.at[slot])

    def pass_on(head, slot, landing, onward, *parts):
        for part in parts:
            arrived(head + part)
            add(slot, *PARTS[part], landing)
            start(onward + part)

    values = node_ref[...].astype(F32)
    inv_rms = lax.rsqrt(jnp.mean(values * values, axis=-1, keepdims=True) + EPSILON)
    mine = pl.ds(pl.multiple_of(core * half, half), half)
    theirs = pl.ds(pl.multiple_of((1 - core) * half, half), half)
    def lend(i, block):
        lent_ref[i] = jnp.concatenate(
            [block, jnp.zeros((padded - rows, half), F32)], axis=0
        ).astype(BF)

    lend(0, node_ref[:, theirs].astype(F32) * inv_rms)
    lend(1, grad_ref[:, theirs].astype(F32))
    pl.semaphore_wait(barrier, len(greet))
    for other in ((after, tp), (after + 1, tp)):
        pl.semaphore_signal(ready_sem, inc=1, device_id=other, device_id_type=MESH)
    start("sn", "sg")
    lend(2, node_ref[:, theirs].astype(F32))
    iv_out[...] = jnp.broadcast_to(inv_rms, iv_out.shape)
    start("nd", "iv")
    raw_up[:, 16] = jnp.zeros((hidden_blocks, U, U), BF)
    raw_down[:, 16] = jnp.zeros((hidden_blocks, U, U), BF)

    def given(i):
        return given_ref[i].astype(F32)[:rows]

    def both(own, other):
        own, other = own.astype(F32), other.astype(F32)
        first = core == 0
        return jnp.concatenate([jnp.where(first, own, other), jnp.where(first, other, own)], axis=0)

    arrived("sn", "sg")
    own_normed = node_ref[:, mine].astype(F32) * inv_rms
    x_ref[0, 0, pl.ds(0, pair)] = both(own_normed.astype(BF), given(0)).astype(BF)
    x_ref[1, 0, pl.ds(0, pair)] = both(grad_ref[:, mine], given(1)).astype(BF)
    start("A1", "A2", "A3a", "A3b", "G0")

    def densify(raw_ref, fill):
        def body(f, _):
            row = pl.ds(pl.multiple_of(f * U, U), U)
            fill(row, [raw_ref[c, kept_ref[c, lax.rem(f + core * 16, 32)]] for c in range(hidden_blocks)])
            return 0

        lax.fori_loop(0, 32, body, 0)

    def fill_up(row, blocks):
        up_ref[row, :] = jnp.concatenate(blocks, axis=1)

    def fill_down(row, blocks):
        down_ref[row, :] = jnp.concatenate(blocks, axis=0).T

    load_up.wait()
    load_down.wait()
    densify(raw_up, fill_up)
    arrived("nd", "iv")
    node_all[...] = both(node_ref[:, mine], given(2)).astype(BF)
    iv_all[...] = both(iv_out[...], iv_in[...])
    densify(raw_down, fill_down)

    wide = min(512, half)
    steps = half // wide

    def compute(begin, height, middle, later):
        r = pl.ds(begin, height)

        def dot(a, b):
            return jnp.dot(a, b, preferred_element_type=F32)

        preact = dot(x_ref[0, 0, r], up_ref[pl.ds(0, half)]) + dot(x_ref[0, 1, r], up_ref[pl.ds(half, half)])
        hidden = dot(x_ref[1, 0, r], down_ref[pl.ds(0, half)]) + dot(x_ref[1, 1, r], down_ref[pl.ds(half, half)])
        s = jax.nn.sigmoid(preact)
        slope = (hidden * s * (1.0 + preact * (1.0 - s))).astype(BF)
        slope_ref[pl.ds(0, height)] = slope
        row_sum = jnp.sum(slope.astype(F32) * preact, axis=-1, keepdims=True) * (1.0 / features)
        row_sum = jnp.broadcast_to(row_sum, (height, U)).astype(BF)
        p_ref[0, r, cols(8, 9)] = row_sum
        p_ref[1, r, cols(8, 9)] = row_sum
        middle()

        def spread(side):
            def body(j, _):
                w = up_ref[pl.ds(pl.multiple_of(side * half + j * wide, wide), wide), :]
                at = j * wide + j // (steps // 2) * U
                part = lax.dot_general(
                    slope_ref[pl.ds(0, height)], w, (((1,), (1,)), ((), ())), preferred_element_type=F32
                )
                p_ref[side, r, pl.ds(pl.multiple_of(at, U), wide)] = part.astype(BF)
                return 0

            lax.fori_loop(0, steps, body, 0)

        spread(1)
        spread(0)
        later()

    arrived("G0")
    compute(0, pair, lambda: None, lambda: start("M1_0"))
    arrived("A1", "A2", "A3a", "A3b")
    start("B1f", "B2f", "C1a", "C2a", "C3", "C4", "G1", "G2", "G3")
    add_sibling(0)
    arrived("G1", "G2", "G3")

    def mid_1():
        start("B1r", "B2r")
        arrived("C1a", "C2a")
        start("E1", "E2")

    compute(pair, 3 * pair, mid_1, lambda: start("M1_1", "M1_2", "M1_3"))
    arrived("B1f", "B2f")
    start("D1", "D2")
    arrived("C3", "B2r")
    arrived("C4", "B1r")
    start("G4", "G5", "C1b", "C2b")
    add_sibling(1, 2, 3)
    start("M2_1", *named("L0", BM), *named("R0", BP))
    arrived("G4", "G5")

    def mid_4():
        arrived("D1", "D2")
        start("G7b")

    def later_4():
        start("M1_4", "M1_5")
        arrived("E1", "E2")
        start("G7a")

    compute(4 * pair, 2 * pair, mid_4, later_4)

    def single(i):
        def before_7():
            add_sibling(4, 5)
            start("M2_4", "M2_5", *named("L1", BM), *named("R1", BP))
            arrived("G7a", "G7b")

        def before_6():
            add_sibling(7)
            start("M2_7", *named("p7", BP), *named("m7", BM))
            arrived("G6")

        def mid_7():
            arrived("C1b", "C2b")
            start("G6")

        def mid_6():
            arrived("M2_4")
            add(2, 0, 8, rr1_ref)
            start(*named("L0", AM))
            arrived("M2_5")
            add(3, 0, 8, r7x_ref)
            start(*named("R0", AP))
            pass_on("p7", 4, r7x_ref, "L1", *BP)
            pass_on("m7", 5, r7x_ref, "R1", *BM)

        def choose(first, second):
            (first, second)[i]()

        choose(before_7, before_6)
        compute(
            (7 - i) * pair, pair,
            lambda: choose(mid_7, mid_6),
            lambda: choose(lambda: start("M1_7"), lambda: start("M1_6")),
        )

    single(0)
    single(1)

    add_sibling(6)
    start("p6Bpa", "m6Bma", "p6Bpb", "m6Bmb")
    arrived("M2_7")
    add(6, 0, 8, r6_ref)
    start("p6Apa", "m6Ama", "p6Apb", "m6Amb")
    arrived("L1Bpa", "L1Bma", "R1Bpa", "R1Bma")
    add(1, 8, 13, rl1_ref, rr1_ref)
    start("M6a")
    pass_on("p6", 2, r6x_ref, "L0", "Bpa")
    pass_on("m6", 3, r6x_ref, "R0", "Bma")
    arrived("L1Bpb", "L1Bmb", "R1Bpb", "R1Bmb")
    add(1, 13, 17, rl1_ref, rr1_ref)
    start("M6b")
    pass_on("p6", 2, r6x_ref, "L0", "Bpb")
    pass_on("m6", 3, r6x_ref, "R0", "Bmb")
    pass_on("p6", 2, r6x_ref, "L0", "Apa")
    pass_on("m6", 3, r6x_ref, "R0", "Ama")
    pass_on("p6", 2, r6x_ref, "L0", "Apb")
    pass_on("m6", 3, r6x_ref, "R0", "Amb")

    inv_all = iv_all[...]

    def finish(unit, *others):
        total = p_ref[0, pl.ds(0, pair), cols(unit, unit + 1)].astype(F32)
        for ref in others:
            total = total + ref[:, cols(unit, unit + 1)].astype(F32)
        return total

    order = (8, 9, 10, 11, 12, 13, 14, 15, 0, 1, 2, 3, 4, 5, 6, 7)

    def emit(place, scaled):
        halves = []
        for unit in order[2 * place : 2 * place + 2]:
            landings = (rl1_ref, rl0_ref, rr0_ref) if unit < 8 else (rl0_ref, rr0_ref, r6_ref)
            at = cols(unit, unit + 1)
            result = x_ref[1, 0, pl.ds(0, pair), at].astype(F32) + inv_all * finish(unit + unit // 8, *landings)
            halves.append(result - node_all[:, at].astype(F32) * scaled)
        for q in range(2):
            both_units = [part[q * rows : (q + 1) * rows] for part in halves]
            fin_ref[q, place] = jnp.concatenate(both_units, axis=0).astype(BF)

    pieces = ((0, 2), (2, 4), (4, 6), (6, 8))

    def shift(piece):
        first, last = pieces[piece]
        copies = []
        for q in range(2):
            copies.append(pltpu.make_async_remote_copy(
                src_ref=fin_ref.at[q, pl.ds(first, last - first)],
                dst_ref=land_ref.at[core, pl.ds(first, last - first)],
                send_sem=send_sem.at[ZSEM + 2 * piece + q],
                recv_sem=recv_sem.at[ZSEM + 2 * piece + core],
                device_id=(before + q, tp), device_id_type=MESH,
            ))
        return copies

    def landed(piece, source):
        first, last = pieces[piece]
        there = land_ref.at[source, pl.ds(first, last - first)]
        pltpu.make_async_remote_copy(
            src_ref=there, dst_ref=there, send_sem=send_sem.at[ZSEM + 2 * piece],
            recv_sem=recv_sem.at[ZSEM + 2 * piece + source], device_id=(before, tp), device_id_type=MESH,
        ).wait_recv()

    def finished(piece, scaled):
        for place in range(*pieces[piece]):
            emit(place, scaled)
        for copy in shift(piece):
            copy.start()

    pl.semaphore_wait(ready_sem, 2)
    arrived("L0Bpa", "L0Bma", "R0Bpa", "R0Bma", "M6a")
    scaled = inv_all * inv_all * finish(8, rl0_ref, rr0_ref, r6_ref)
    finished(0, scaled)
    arrived("L0Bpb", "L0Bmb", "R0Bpb", "R0Bmb", "M6b")
    finished(1, scaled)
    arrived("M2_1", "L0Ama", "L0Apa", "R0Ama", "R0Apa")
    finished(2, scaled)
    arrived("L0Amb", "L0Apb", "R0Amb", "R0Apb")
    finished(3, scaled)

    for piece, (first, last) in enumerate(pieces):
        for source in range(2):
            landed(piece, source)
            for place in range(first, last):
                units = land_ref[source, place].astype(F32)
                for i, unit in enumerate(order[2 * place : 2 * place + 2]):
                    at = pl.ds(source * half + unit * U, U)
                    out_ref[:, at] = units[i * rows : (i + 1) * rows].astype(BF)
    for name in NAMES:
        remote(name).wait_send()
    for piece in range(len(pieces)):
        for copy in shift(piece):
            copy.wait_send()


def body(layers, node_rows, out_grad, up_blocks, down_blocks, block_rows):
    rows, features = node_rows.shape
    hidden_blocks, kept = block_rows.shape
    pair, half, hidden = 2 * rows, features // 2, hidden_blocks * U
    padded = (rows + 15) // 16 * 16
    wanted = block_rows[:, None, :] == jnp.arange(features // U, dtype=jnp.int32)[None, :, None]
    inverse = jnp.min(jnp.where(wanted, jnp.arange(kept, dtype=jnp.int32), kept), axis=-1)

    def vmem(*shape, dtype=BF):
        return pltpu.VMEM(shape, dtype)

    in_vmem = pl.BlockSpec(memory_space=pltpu.VMEM)
    return pl.pallas_call(
        functools.partial(kernel, rows, layers),
        out_shape=jax.ShapeDtypeStruct((rows, features), BF),
        in_specs=[
            pl.BlockSpec(memory_space=pltpu.SMEM), in_vmem, in_vmem,
            pl.BlockSpec(memory_space=pl.ANY), pl.BlockSpec(memory_space=pl.ANY),
        ],
        out_specs=in_vmem,
        scratch_shapes=[
            vmem(2, 2, TP * pair, half),
            vmem(features, hidden),
            vmem(features, hidden),
            vmem(hidden_blocks, kept + 1, U, U),
            vmem(hidden_blocks, kept + 1, U, U),
            vmem(3 * pair, hidden),
            vmem(2, TP * pair, PU * U),
            vmem(8, pair, PU * U),
            *[vmem(pair, PU * U) for _ in range(7)],
            vmem(3, padded, half),
            vmem(3, padded, half),
            vmem(rows, U, dtype=F32),
            vmem(rows, U, dtype=F32),
            vmem(pair, half),
            vmem(pair, U, dtype=F32),
            vmem(2, HU // 2, pair, U),
            vmem(2, HU // 2, pair, U),
            pltpu.SemaphoreType.DMA((ZSEM + 8,)),
            pltpu.SemaphoreType.DMA((ZSEM + 8,)),
            pltpu.SemaphoreType.DMA((2,)),
            pltpu.SemaphoreType.REGULAR,
        ],
        compiler_params=pltpu.CompilerParams(
            collective_id=0, has_side_effects=True, vmem_limit_bytes=62 * 2**20
        ),
        name="layer_grad",
    )(inverse, node_rows, out_grad, up_blocks, down_blocks)


def solution(mesh):
    layers = mesh.shape["segment"] // 2
    return jax.shard_map(
        functools.partial(body, layers),
        mesh=mesh,
        in_specs=(
            P(("segment", "tp"), None),
            P(("segment", "tp"), None),
            P(("segment", "tp"), None, None, None),
            P(("segment", "tp"), None, None, None),
            P(("segment", "tp"), None),
        ),
        out_specs=P(("segment", "tp"), None),
        check_vma=False,
    )
```
